256 devices in a mesh: seq: 128 (over z, x, y_hi, core), head: 2 (over y_lo).
Axes of the slice: x: 4, y: 4 (y_hi: 2, y_lo: 2; y = y_hi * 2 + y_lo), z: 8, core: 2. Of those that a mesh axis runs over, the one named last changes fastest.
Arguments:
- image_query: bfloat16 [16, 16, 1024, 128], P(None, 'head', 'seq'), may hold values from -120 to 120
- image_key: bfloat16 [16, 16, 1024, 128], P(None, 'head', 'seq'), may hold values from -7 to 7
- image_value: bfloat16 [16, 16, 1024, 128], P(None, 'head', 'seq'), may hold values from -6 to 6
- text_query: bfloat16 [16, 16, 512, 128], P(None, 'head', 'seq'), may hold values from -6 to 6
- text_key: bfloat16 [16, 16, 512, 128], P(None, 'head', 'seq'), may hold values from -6 to 6
- text_value: bfloat16 [16, 16, 512, 128], P(None, 'head', 'seq'), may hold values from -6 to 6
- out_weight: bfloat16 [2048, 3072], P('head'), may hold values from -0.125 to 0.125
- image_count: int32 [16], replicated, may hold values from 256 to 1024, as said below
- text_length: int32 [16], replicated, may hold values from 64 to 512, as said below
Outputs:
- image_out: bfloat16 [16, 1024, 3072], P('head', 'seq')
- text_out: bfloat16 [16, 512, 3072], P('head', 'seq')
The draws below stay inside these ranges and needn't reach their ends.
Inputs may be any that keep to these rules, and one draw needn't show every extreme that they name: `image_count`: in every draw some image has all 1024 tokens valid. `text_length`: in every draw some image has all 512 text tokens valid.
All inputs are finite; a program needn't handle non-finite values.
Results may differ from the reference program's by a relative error of at most 0.012.
Values may be sent and summed in bfloat16 or wider, within the bound.
A program may use at most 64 MiB of HBM per device.

```python
import jax
import jax.numpy as jnp
from jax import lax

D = 3072
HEADS = 16
HD = 128
TXT = 512
IMG_TOK = 1024
IMAGES = 16


def bounded_normal(key, shape):
    return jax.random.truncated_normal(key, -6.0, 6.0, shape, jnp.float32)


def key_base(key):
    return bounded_normal(key, (IMAGES, HEADS, IMG_TOK, HD))


def draw_image_key(key, part):
    base = key_base(key)
    return base.astype(jnp.bfloat16)


def draw_image_query(key, part):
    base = key_base(key)
    key = jax.random.fold_in(key, 17)
    fresh = bounded_normal(key, base.shape)
    return fresh.astype(jnp.bfloat16)


def draw_image_count(key, part):
    key = jax.random.fold_in(key, 23)
    key_draw, key_pick = jax.random.split(key)
    lengths = jax.random.randint(key_draw, (IMAGES,), IMG_TOK // 4, IMG_TOK + 1)
    fullest = jax.random.randint(key_pick, (), 0, IMAGES)
    return jnp.where(jnp.arange(IMAGES) == fullest, IMG_TOK, lengths).astype(jnp.int32)


def draw_text_length(key, part):
    key = jax.random.fold_in(key, 29)
    key_draw, key_pick = jax.random.split(key)
    lengths = jax.random.randint(key_draw, (IMAGES,), TXT // 8, TXT + 1)
    fullest = jax.random.randint(key_pick, (), 0, IMAGES)
    return jnp.where(jnp.arange(IMAGES) == fullest, TXT, lengths).astype(jnp.int32)


def block_levels(stream_key, dims, pieces, smallest, high):
    loudness, own = 1.0, jax.random.fold_in(stream_key, 6)
    for axis_at, shards_of in pieces:
        steps = jnp.exp(jax.random.uniform(jax.random.fold_in(own, axis_at), (shards_of,), jnp.float32, smallest / len(pieces), high / len(pieces)))
        loudness = loudness * jnp.repeat(steps, dims[axis_at] // shards_of).reshape([-1 if axis == axis_at else 1 for axis in range(len(dims))])
    return loudness


def centred(rng, extent, deviation, bound, cuts=(), held_as=jnp.bfloat16):
    factor_of = block_levels(rng, extent, cuts, -0.22, 0.18) if cuts else 1.0
    drawn = jax.random.normal(rng, extent, jnp.float32) * deviation * factor_of
    return jnp.minimum(jnp.maximum(drawn, -bound), bound).astype(held_as)


def setup_inputs(seed: int = 0) -> dict:
    key_list = jax.random.split(jax.random.key(seed), 10)
    return {
        "image_query": draw_image_query(jax.random.fold_in(key_list[9], 71), 0),
        "image_key": draw_image_key(jax.random.fold_in(key_list[9], 71), 0),
        "image_value": centred(key_list[2], (IMAGES, HEADS, IMG_TOK, HD), 1.0, 6.0, ((1, 2), (2, 128))),
        "text_query": centred(key_list[3], (IMAGES, HEADS, TXT, HD), 1.0, 6.0, ((1, 2), (2, 128))),
        "text_key": centred(key_list[4], (IMAGES, HEADS, TXT, HD), 1.0, 6.0, ((1, 2), (2, 128))),
        "text_value": centred(key_list[5], (IMAGES, HEADS, TXT, HD), 1.0, 6.0, ((1, 2), (2, 128))),
        "out_weight": centred(key_list[6], (HEADS * HD, D), (HEADS * HD) ** -0.5, 0.125, ((0, 2),)),
        "image_count": draw_image_count(jax.random.fold_in(key_list[9], 71), 0),
        "text_length": draw_text_length(jax.random.fold_in(key_list[9], 71), 0),
    }


def attend_pair(queries, keys, values, key_valid):
    scores = jnp.dot(queries, keys.T, preferred_element_type=jnp.float32) * (HD ** -0.5)
    scores = jnp.where(key_valid[None, :], scores, -jnp.inf)
    highest = jnp.max(scores, axis=1, keepdims=True)
    powers = jnp.exp(scores - highest)
    shares = powers / jnp.sum(powers, axis=1, keepdims=True)
    weights_low = shares.astype(jnp.bfloat16)
    return jnp.dot(weights_low, values, preferred_element_type=jnp.float32).astype(jnp.bfloat16)


def reference(image_query, image_key, image_value, text_query, text_key, text_value, out_weight, image_count, text_length):
    joint_query = jnp.concatenate([text_query, image_query], axis=2)
    joint_key = jnp.concatenate([text_key, image_key], axis=2)
    joint_value = jnp.concatenate([text_value, image_value], axis=2)
    positions = jnp.arange(TXT + IMG_TOK, dtype=jnp.int32)

    def one_pair(pair_index):
        image_index = pair_index // HEADS
        head_index = pair_index % HEADS
        key_valid = jnp.where(positions < TXT, positions < text_length[image_index], positions - TXT < image_count[image_index])
        return attend_pair(joint_query[image_index, head_index], joint_key[image_index, head_index], joint_value[image_index, head_index], key_valid)

    attended = lax.map(one_pair, jnp.arange(IMAGES * HEADS, dtype=jnp.int32))
    attended = attended.reshape(IMAGES, HEADS, TXT + IMG_TOK, HD)
    weight_heads = out_weight.reshape(HEADS, HD, D).astype(jnp.float32)

    def project(image_block):
        return jnp.einsum("htd,hdo->to", image_block.astype(jnp.float32), weight_heads).astype(jnp.bfloat16)

    projected = lax.map(project, attended)
    return projected[:, TXT:], projected[:, :TXT]
```

```python
import functools

import jax
import jax.numpy as jnp
from jax import lax
from jax.experimental import pallas as pl
from jax.experimental.pallas import tpu as pltpu
from jax.sharding import PartitionSpec as P

MESH = pl.DeviceIdType.MESH
BF16 = jnp.bfloat16
F32 = jnp.float32

PLANES = 8
SLOTS = 16
HD = 128
IT, TT = 8, 4
CHUNK = SLOTS * (IT + TT)
IMG_KEYS = PLANES * SLOTS * IT
TXT_KEYS = PLANES * SLOTS * TT
KEYS = IMG_KEYS + TXT_KEYS
ROWS = 48
COLS = 512


def merge(block):
    wide = block.astype(F32)
    rows = 1
    for extent in block.shape[:-1]:
        rows *= extent
    return wide.reshape(rows, block.shape[-1]).astype(BF16)


def kernel(
    iq, ik, iv, tq, tk, tv, weight, counts, lengths,
    out_image, out_text,
    a_ik, a_tk, a_iq, a_tq, a_iv, a_tv,
    b_ik, b_tk, b_iq, b_tq, b_iv, b_tv,
    keys, values, powers, inverse,
    s_img, s_txt, c_img, c_txt, d_img, d_txt,
    w_vmem, lhs, part_send, part_recv, part_own,
    a_send, a_recv, b_send, b_recv, c_send, c_recv, d_send, d_recv,
    y_send, y_recv, w_sem, own_sem,
):
    seq = lax.axis_index("seq")
    eta = lax.axis_index("head")
    z, q = seq // SLOTS, seq % SLOTS
    width = weight.shape[1]
    steps = width // COLS

    def plane_peer(step):
        qx = (q // 4 + step // 4) % 4
        qy = ((q // 2) % 2 + (step // 2) % 2) % 2
        qc = (q % 2 + step % 2) % 2
        return qx * 4 + qy * 2 + qc

    def flipped(slot):
        return slot + 2 - 4 * ((slot // 2) % 2)

    def z_device(plane):
        return (plane * SLOTS + q, eta)

    def q_device(slot):
        return (z * SLOTS + slot, eta)

    partner_direct = (seq, 1 - eta)
    partner_flipped = (z * SLOTS + flipped(q), 1 - eta)

    barrier = pltpu.get_barrier_semaphore()

    def greet_z(step, carry):
        pl.semaphore_signal(
            barrier, inc=1, device_id=z_device((z + step) % PLANES), device_id_type=MESH
        )
        return carry

    def greet_q(step, carry):
        pl.semaphore_signal(
            barrier, inc=1, device_id=q_device(plane_peer(step)), device_id_type=MESH
        )
        return carry

    lax.fori_loop(1, PLANES, greet_z, 0)
    lax.fori_loop(1, SLOTS, greet_q, 0)
    pl.semaphore_signal(barrier, inc=1, device_id=partner_direct, device_id_type=MESH)
    pl.semaphore_signal(barrier, inc=1, device_id=partner_flipped, device_id_type=MESH)
    pl.semaphore_wait(barrier, PLANES - 1 + SLOTS - 1 + 2)

    def remote(src, dst, send, recv, device):
        return pltpu.make_async_remote_copy(
            src_ref=src, dst_ref=dst, send_sem=send, recv_sem=recv,
            device_id=device, device_id_type=MESH,
        )

    first = ((ik, a_ik), (tk, a_tk), (iq, a_iq), (tq, a_tq), (iv, a_iv), (tv, a_tv))
    second = (b_ik, b_tk, b_iq, b_tq, b_iv, b_tv)

    def start_a(n):
        src, dst = first[n]

        def body(step, carry):
            plane = (z + step) % PLANES
            remote(
                src.at[plane], dst.at[z], a_send.at[n], a_recv.at[n], z_device(plane)
            ).start()
            return carry

        lax.fori_loop(1, PLANES, body, 0)
        pltpu.make_async_copy(src.at[z], dst.at[z], own_sem.at[n]).start()

    def wait_a(n):
        src, dst = first[n]
        some = dst.at[pl.ds(0, PLANES - 1)]
        remote(some, some, a_send.at[n], a_recv.at[n], z_device(z)).wait_recv()
        pltpu.make_async_copy(src.at[z], dst.at[z], own_sem.at[n]).wait()

    def start_b(n):
        src, dst = first[n][1], second[n]

        def body(step, carry):
            slot = plane_peer(step)
            remote(
                src.at[:, slot], dst.at[:, q], b_send.at[n], b_recv.at[n], q_device(slot)
            ).start()
            return carry

        lax.fori_loop(1, SLOTS, body, 0)
        pltpu.make_async_copy(src.at[:, q], dst.at[:, q], own_sem.at[6 + n]).start()

    def wait_b(n):
        src, dst = first[n][1], second[n]
        some = dst.at[:, pl.ds(0, SLOTS - 1)]
        remote(some, some, b_send.at[n], b_recv.at[n], q_device(q)).wait_recv()
        pltpu.make_async_copy(src.at[:, q], dst.at[:, q], own_sem.at[6 + n]).wait()

    for n in range(6):
        start_a(n)
    load = pltpu.make_async_copy(weight, w_vmem, w_sem)
    load.start()
    for n in range(4):
        wait_a(n)
        start_b(n)

    image = 2 * z + q // 8
    count, length = counts[image], lengths[image]
    position = lax.broadcasted_iota(jnp.int32, (1, KEYS), 1)
    limit = jnp.where(position < IMG_KEYS, count, IMG_KEYS + length)
    bias = jnp.where(position < limit, 0.0, -1e30).astype(F32)

    wait_b(0)
    wait_b(1)
    keys[0:IMG_KEYS] = merge(b_ik[...])
    keys[IMG_KEYS:KEYS] = merge(b_tk[...])
    wait_b(2)
    wait_b(3)

    factor = HD**-0.5 * 1.4426950408889634

    def score(chunk, carry):
        rows = jnp.concatenate([merge(b_iq[chunk]), merge(b_tq[chunk])], axis=0)
        scores = lax.dot_general(
            rows, keys[...], (((1,), (1,)), ((), ())), preferred_element_type=F32
        )
        scores = scores + bias
        highest = jnp.max(scores, axis=1, keepdims=True)
        power = jnp.exp2((scores - highest) * factor)
        total = jnp.sum(power, axis=1, keepdims=True)
        powers[chunk] = power.astype(BF16)
        inverse[chunk] = jnp.broadcast_to(1.0 / total, (CHUNK, HD))
        return carry

    lax.fori_loop(0, PLANES, score, 0)

    for n in (4, 5):
        wait_a(n)
        start_b(n)
    wait_b(4)
    wait_b(5)
    values[0:IMG_KEYS] = merge(b_iv[...])
    values[IMG_KEYS:KEYS] = merge(b_tv[...])

    def attend(plane):
        mixed = jnp.dot(powers[plane], values[...], preferred_element_type=F32)
        mixed = mixed * inverse[plane]
        image_rows = mixed[0 : SLOTS * IT].reshape(SLOTS, IT, HD).astype(BF16)
        text_rows = mixed[SLOTS * IT : CHUNK].reshape(SLOTS, TT, HD).astype(BF16)
        return image_rows, text_rows

    def send_back(step, carry):
        plane = (z + step) % PLANES
        image_rows, text_rows = attend(plane)
        s_img[plane] = image_rows
        s_txt[plane] = text_rows
        remote(
            s_img.at[plane], c_img.at[z], c_send.at[0], c_recv.at[0], z_device(plane)
        ).start()
        remote(
            s_txt.at[plane], c_txt.at[z], c_send.at[1], c_recv.at[1], z_device(plane)
        ).start()
        return carry

    lax.fori_loop(1, PLANES, send_back, 0)
    image_rows, text_rows = attend(z)
    c_img[z] = image_rows
    c_txt[z] = text_rows

    near, far = 2 * eta, 6 - 6 * eta

    def ranges(src, dst, slot):
        return (
            (src.at[pl.ds(near, 6), slot], dst.at[q, pl.ds(near, 6)]),
            (src.at[pl.ds(far, 2), flipped(slot)], dst.at[q, pl.ds(far, 2)]),
        )

    for n, (src, dst) in enumerate(((c_txt, d_txt), (c_img, d_img))):
        m = 1 - n
        some = src.at[pl.ds(0, PLANES - 1)]
        remote(some, some, c_send.at[m], c_recv.at[m], z_device(z)).wait_recv()

        def share(step, carry, src=src, dst=dst, n=n):
            slot = plane_peer(step)
            for a, b in ranges(src, dst, slot):
                remote(a, b, d_send.at[n], d_recv.at[n], q_device(slot)).start()
            return carry

        lax.fori_loop(1, SLOTS, share, 0)
        for m, (a, b) in enumerate(ranges(src, dst, q)):
            pltpu.make_async_copy(a, b, own_sem.at[12 + 2 * n + m]).start()
    load.wait()
    for n, (src, dst) in enumerate(((c_txt, d_txt), (c_img, d_img))):
        some = dst.at[pl.ds(0, SLOTS - 1)]
        remote(some, some, d_send.at[n], d_recv.at[n], q_device(q)).wait_recv()
        for m, (a, b) in enumerate(ranges(src, dst, q)):
            pltpu.make_async_copy(a, b, own_sem.at[12 + 2 * n + m]).wait()

    bases = ((4 - 2 * eta, far), (2 + 2 * eta, 6 * eta))
    for side in range(2):
        for half in range(2):
            base = bases[side][half]
            for head in range(8):
                rows = jnp.concatenate(
                    [
                        d_img[parity * 8 + head, pl.ds(base, 2)].astype(F32).reshape(16, HD)
                        for parity in range(2)
                    ]
                    + [
                        d_txt[parity * 8 + head, pl.ds(base, 2)].astype(F32).reshape(8, HD)
                        for parity in range(2)
                    ],
                    axis=0,
                )
                lhs[
                    side, half * ROWS : (half + 1) * ROWS, head * HD : (head + 1) * HD
                ] = rows.astype(BF16)

    for step in range(steps):
        columns = pl.ds(step * COLS, COLS)
        part = jnp.dot(lhs[0], w_vmem[:, columns], preferred_element_type=F32)
        part_send[step] = part.astype(BF16).reshape(2, ROWS, COLS)
        for half, device in enumerate((partner_direct, partner_flipped)):
            remote(
                part_send.at[step, half], part_recv.at[step, half],
                y_send.at[step, half], y_recv.at[step, half], device,
            ).start()
    for step in range(steps):
        columns = pl.ds(step * COLS, COLS)
        part_own[step] = jnp.dot(lhs[1], w_vmem[:, columns], preferred_element_type=F32)

    firsts = (4 - 4 * eta, 4 * eta)
    for step in range(steps):
        columns = pl.ds(step * COLS, COLS)
        for half, device in enumerate((partner_direct, partner_flipped)):
            remote(
                part_send.at[step, half], part_recv.at[step, half],
                y_send.at[step, half], y_recv.at[step, half], device,
            ).wait()
            total = part_own[step, half * ROWS : (half + 1) * ROWS] + part_recv[
                step, half
            ].astype(F32)
            for parity in range(2):
                for near_z in range(2):
                    at = firsts[half] + 2 * near_z + parity
                    row = parity * 16 + near_z * 8
                    out_image[at, :, columns] = total[row : row + 8].astype(BF16)
                    row = 32 + parity * 8 + near_z * 4
                    out_text[at, :, columns] = total[row : row + 4].astype(BF16)

    for n in range(6):
        src, dst = first[n]
        some = dst.at[pl.ds(0, PLANES - 1)]
        remote(some, some, a_send.at[n], a_recv.at[n], z_device(z)).wait_send()
        some = second[n].at[:, pl.ds(0, SLOTS - 1)]
        remote(some, some, b_send.at[n], b_recv.at[n], q_device(q)).wait_send()
    for m, (src, dst) in enumerate(((c_img, d_img), (c_txt, d_txt))):
        some = src.at[pl.ds(0, PLANES - 1)]
        remote(some, some, c_send.at[m], c_recv.at[m], z_device(z)).wait_send()
        some = dst.at[pl.ds(0, SLOTS - 1)]
        remote(some, some, d_send.at[1 - m], d_recv.at[1 - m], q_device(q)).wait_send()


def body(iq, ik, iv, tq, tk, tv, weight, counts, lengths):
    width = weight.shape[1]
    steps = width // COLS

    def planes(tensor):
        return tensor.reshape(PLANES, SLOTS, tensor.shape[2], HD)

    img = pltpu.VMEM((PLANES, SLOTS, IT, HD), BF16)
    txt = pltpu.VMEM((PLANES, SLOTS, TT, HD), BF16)
    dma = pltpu.SemaphoreType.DMA
    anywhere = pl.BlockSpec(memory_space=pl.ANY)
    scalars = pl.BlockSpec(memory_space=pltpu.SMEM)
    vmem = pl.BlockSpec(memory_space=pltpu.VMEM)
    return pl.pallas_call(
        kernel,
        out_shape=(
            jax.ShapeDtypeStruct((8, IT, width), BF16),
            jax.ShapeDtypeStruct((8, TT, width), BF16),
        ),
        in_specs=[anywhere] * 7 + [scalars] * 2,
        out_specs=(vmem, vmem),
        scratch_shapes=[
            *([img, txt] * 3),
            *([img, txt] * 3),
            pltpu.VMEM((KEYS, HD), BF16),
            pltpu.VMEM((KEYS, HD), BF16),
            pltpu.VMEM((PLANES, CHUNK, KEYS), BF16),
            pltpu.VMEM((PLANES, CHUNK, HD), F32),
            img, txt, img, txt,
            pltpu.VMEM((SLOTS, PLANES, IT, HD), BF16),
            pltpu.VMEM((SLOTS, PLANES, TT, HD), BF16),
            pltpu.VMEM(weight.shape, BF16),
            pltpu.VMEM((2, 2 * ROWS, 8 * HD), BF16),
            pltpu.VMEM((steps, 2, ROWS, COLS), BF16),
            pltpu.VMEM((steps, 2, ROWS, COLS), BF16),
            pltpu.VMEM((steps, 2 * ROWS, COLS), F32),
            dma((6,)), dma((6,)), dma((6,)), dma((6,)),
            dma((2,)), dma((2,)), dma((2,)), dma((2,)),
            dma((steps, 2)), dma((steps, 2)), dma, dma((16,)),
        ],
        compiler_params=pltpu.CompilerParams(
            collective_id=0, has_side_effects=True, vmem_limit_bytes=48 * 2**20
        ),
        cost_estimate=pl.CostEstimate(
            flops=2_500_000_000, bytes_accessed=10_000_000, transcendentals=2_400_000
        ),
        name="joint_attention",
    )(planes(iq), planes(ik), planes(iv), planes(tq), planes(tk), planes(tv), weight, counts, lengths)


def solution(mesh):
    tokens = P(None, "head", "seq", None)
    return jax.shard_map(
        body,
        mesh=mesh,
        in_specs=(tokens,) * 6 + (P("head", None), P(), P()),
        out_specs=(P("head", "seq", None), P("head", "seq", None)),
        check_vma=False,
    )
```

```python
import jax
import jax.numpy as jnp
from jax import lax
from jax.experimental import pallas as pl
from jax.experimental.pallas import tpu as pltpu
from jax.sharding import PartitionSpec as P

MESH = pl.DeviceIdType.MESH
BF16 = jnp.bfloat16
F32 = jnp.float32

PLANES = 8
SLOTS = 16
HD = 128
IT, TT = 8, 4
IMG_KEYS = PLANES * SLOTS * IT
TXT_KEYS = PLANES * SLOTS * TT
KEYS = IMG_KEYS + TXT_KEYS
COLS = 1024


def merge(block):
    wide = block.astype(F32)
    rows = 1
    for extent in block.shape[:-1]:
        rows *= extent
    return wide.reshape(rows, block.shape[-1]).astype(BF16)


def kernel(
    iq, ik, iv, tq, tk, tv, weight, counts_hbm, lengths_hbm,
    out_image, out_text,
    a_ik, a_tk, a_iv, a_tv, a_iq, a_tq,
    b_ik, b_tk, b_iv, b_tv, b_iq, b_tq,
    keys, values,
    s_img, s_txt, c_img, c_txt, other_img, other_txt, own_img, own_txt,
    w_vmem, lhs_img, lhs_txt, lhs_own,
    send_img, send_txt, recv_img, recv_txt, part_own,
    counts, lengths,
    v_ik, v_tk, v_iv, v_tv, v_iq, v_tq, load_sem,
    a_send, a_recv, b_send, b_recv, c_send, c_recv, d_send, d_recv,
    y_send, y_recv, w_sem, own_sem,
):
    seq = lax.axis_index("seq")
    eta = lax.axis_index("head")
    z = seq // SLOTS
    x, y, c = (seq // 4) % 4, (seq // 2) % 2, seq % 2
    pos = x * 2 + c
    slot = y * 8 + pos
    steps = weight.shape[1] // COLS

    def plane_peer(step):
        return (x + step // 4) % 4, (y + (step // 2) % 2) % 2, (c + step % 2) % 2

    def ring(step):
        return (z + 4 + (step // 2) * (2 * (step % 2) - 1)) % PLANES

    def device(plane, place):
        px, py, pc = place
        return (plane * SLOTS + px * 4 + py * 2 + pc, eta)

    here = (x, y, c)
    planes = [ring(step) for step in range(1, PLANES)]
    places = [plane_peer(step) for step in range(1, SLOTS)]
    row_places = [((x + step // 2) % 4, y, (c + step % 2) % 2) for step in range(1, 8)]

    def z_device(plane):
        return device(plane, here)

    def q_device(place):
        return device(z, place)

    def slot_of(place):
        px, py, pc = place
        return py * 8 + px * 2 + pc

    partners = ((seq, 1 - eta), (seq + 2 - 4 * y, 1 - eta))

    sources = ((ik, v_ik), (tk, v_tk), (iv, v_iv), (tv, v_tv), (iq, v_iq), (tq, v_tq))
    loads = [
        pltpu.make_async_copy(src, dst, load_sem.at[n])
        for n, (src, dst) in enumerate(sources)
    ]
    for copy in loads:
        copy.start()

    barrier = pltpu.get_barrier_semaphore()
    peers = [z_device(plane) for plane in planes]
    peers += [q_device(place) for place in places]
    peers += partners
    for peer in peers:
        pl.semaphore_signal(barrier, inc=1, device_id=peer, device_id_type=MESH)
    pl.semaphore_wait(barrier, len(peers))

    arrivals, departures = {}, []

    def remote(src, dst, send, recv, device):
        return pltpu.make_async_remote_copy(
            src_ref=src, dst_ref=dst, send_sem=send, recv_sem=recv,
            device_id=device, device_id_type=MESH,
        )

    def local(name, src, dst, sem):
        copy = pltpu.make_async_copy(src, dst, sem)
        copy.start()
        arrivals.setdefault(name, []).append(copy.wait)

    def expect(name, some, send, recv):
        copy = remote(some, some, send, recv, partners[0])
        arrivals.setdefault(name, []).append(copy.wait_recv)
        departures.append(copy.wait_send)

    def arrive(name):
        for wait in arrivals.pop(name):
            wait()


    first = ((v_ik, a_ik), (v_tk, a_tk), (v_iv, a_iv), (v_tv, a_tv), (v_iq, a_iq), (v_tq, a_tq))
    second = (b_ik, b_tk, b_iv, b_tv, b_iq, b_tq)

    def start_a(n):
        loads[n].wait()
        src, dst = first[n]
        for plane in planes:
            remote(
                src.at[plane], dst.at[z], a_send.at[n], a_recv.at[n], z_device(plane)
            ).start()
        expect(("a", n), dst.at[pl.ds(0, PLANES - 1)], a_send.at[n], a_recv.at[n])
        local(("a", n), src.at[z], dst.at[z], own_sem.at[n])

    def start_b(n):
        src, dst = first[n][1], second[n]
        for place in places:
            remote(
                src.at[:, slot_of(place)], dst.at[:, slot],
                b_send.at[n], b_recv.at[n], q_device(place),
            ).start()
        expect(("b", n), dst.at[:, pl.ds(0, SLOTS - 1)], b_send.at[n], b_recv.at[n])
        local(("b", n), src.at[:, slot], dst.at[:, slot], own_sem.at[6 + n])

    for n in range(2):
        start_a(n)
    local("weight", weight, w_vmem, w_sem)
    local("scalars", counts_hbm, counts, own_sem.at[16])
    local("scalars", lengths_hbm, lengths, own_sem.at[17])

    for n in range(4):
        arrive(("a", n))
        if n < 3:
            start_a(n + 2)
        start_b(n)

    arrive("scalars")
    image = 2 * z + y
    count, length = counts[image], lengths[image]

    def valid(extent, rows, limit):
        index = lax.broadcasted_iota(jnp.int32, (1, extent), 1)
        at = (index // rows) % SLOTS
        owner = index // (rows * SLOTS) * SLOTS + (at // 2) % 4 * 4 + at // 8 * 2 + at % 2
        return owner * rows + index % rows < limit

    bias = jnp.concatenate(
        [
            jnp.where(valid(IMG_KEYS, IT, count), 0.0, -1e30),
            jnp.where(valid(TXT_KEYS, TT, length), 0.0, -1e30),
        ],
        axis=1,
    ).astype(F32)

    arrive(("b", 0))
    keys[0:IMG_KEYS] = merge(b_ik[...])
    arrive(("b", 1))
    keys[IMG_KEYS:KEYS] = merge(b_tk[...])
    arrive(("b", 2))
    values[0:IMG_KEYS] = merge(b_iv[...])
    arrive(("b", 3))
    values[IMG_KEYS:KEYS] = merge(b_tv[...])

    factor = HD**-0.5 * 1.4426950408889634

    def attend(rows):
        scores = lax.dot_general(
            rows, keys[...], (((1,), (1,)), ((), ())), preferred_element_type=F32
        )
        scores = scores + bias
        highest = jnp.max(scores, axis=1, keepdims=True)
        powers = jnp.exp2((scores - highest) * factor)
        total = jnp.sum(powers, axis=1, keepdims=True)
        mixed = jnp.dot(powers.astype(BF16), values[...], preferred_element_type=F32)
        return mixed * (1.0 / total)

    arrive(("a", 4))
    start_b(4)
    start_a(5)
    arrive(("b", 4))
    arrive(("a", 5))
    start_b(5)

    def image_chunk(step, carry):
        plane = ring(step)
        mixed = attend(merge(b_iq[plane]))
        s_img[plane] = mixed.reshape(2, 8, IT, HD).astype(BF16)
        remote(
            s_img.at[plane], c_img.at[z], c_send.at[0], c_recv.at[0], z_device(plane)
        ).start()
        return carry

    lax.fori_loop(1, PLANES, image_chunk, 0)
    expect(("c", 0), c_img.at[pl.ds(0, PLANES - 1)], c_send.at[0], c_recv.at[0])
    c_img[z] = attend(merge(b_iq[z])).reshape(2, 8, IT, HD).astype(BF16)

    arrive(("b", 5))

    def text_pair(planes):
        rows = [merge(b_tq[plane]) for plane in planes]
        return attend(jnp.concatenate(rows, axis=0)).reshape(2, 2, 8, TT, HD).astype(BF16)

    def send_text(plane, mixed):
        s_txt[plane] = mixed
        remote(
            s_txt.at[plane], c_txt.at[z], c_send.at[1], c_recv.at[1], z_device(plane)
        ).start()

    def text_chunk(step, carry):
        pair = [ring(2 * step + 1 + k) for k in range(2)]
        mixed = text_pair(pair)
        for k in range(2):
            send_text(pair[k], mixed[k])
        return carry

    lax.fori_loop(0, 3, text_chunk, 0)
    mixed = text_pair((planes[6], z))
    send_text(planes[6], mixed[0])
    c_txt[z] = mixed[1]
    expect(("c", 1), c_txt.at[pl.ds(0, PLANES - 1)], c_send.at[1], c_recv.at[1])

    mine, others = pl.ds(4 * eta, 4), pl.ds(4 - 4 * eta, 4)
    spread = ((c_img, other_img, own_img), (c_txt, other_txt, own_txt))
    for n, (src, other, own) in enumerate(spread):
        arrive(("c", n))
        for place in row_places:
            remote(
                src.at[others, :, place[0] * 2 + place[2]], other.at[pos],
                d_send.at[n], d_recv.at[n], q_device(place),
            ).start()
        expect(("d", n), other.at[pl.ds(0, 7)], d_send.at[n], d_recv.at[n])
        local(("d", n), src.at[others, :, pos], other.at[pos], own_sem.at[12 + n])
        for place in places:
            remote(
                src.at[mine, place[1], place[0] * 2 + place[2]], own.at[slot],
                d_send.at[2 + n], d_recv.at[2 + n], q_device(place),
            ).start()
        expect(("d", 2 + n), own.at[pl.ds(0, SLOTS - 1)], d_send.at[2 + n], d_recv.at[2 + n])
        local(("d", 2 + n), src.at[mine, y, pos], own.at[slot], own_sem.at[14 + n])

    arrive("weight")
    sides = (y, 1 - y)
    partial = (
        (other_img, lhs_img, send_img, recv_img), (other_txt, lhs_txt, send_txt, recv_txt)
    )
    for n, (other, lhs, send, recv) in enumerate(partial):
        height = lhs.shape[0] // 2
        arrive(("d", n))
        for half in range(2):
            for head in range(8):
                lhs[
                    half * height : (half + 1) * height, head * HD : (head + 1) * HD
                ] = merge(other[head, :, sides[half]])
        for step in range(steps):
            columns = pl.ds(step * COLS, COLS)
            part = jnp.dot(lhs[...], w_vmem[:, columns], preferred_element_type=F32)
            send[step] = part.astype(BF16).reshape(2, height, COLS)
            for half, partner in enumerate(partners):
                copy = remote(
                    send.at[step, half], recv.at[step, half],
                    y_send.at[n, step, half], y_recv.at[n, step, half], partner,
                )
                copy.start()
                arrivals[("y", n, step, half)] = [copy.wait_recv]
                departures.append(copy.wait_send)

    for n, (own, first_row, height) in enumerate(((own_img, 0, 4 * IT), (own_txt, 8 * IT, 4 * TT))):
        arrive(("d", 2 + n))
        for half in range(2):
            start = first_row + half * height
            for head in range(8):
                lhs_own[start : start + height, head * HD : (head + 1) * HD] = merge(
                    own[sides[half] * 8 + head]
                )
    for step in range(steps):
        columns = pl.ds(step * COLS, COLS)
        part_own[step] = jnp.dot(lhs_own[...], w_vmem[:, columns], preferred_element_type=F32)

    for n, (recv, out, first_row, rows) in enumerate(
        ((recv_img, out_image, 0, IT), (recv_txt, out_text, 8 * IT, TT))
    ):
        for step in range(steps):
            columns = pl.ds(step * COLS, COLS)
            for half in range(2):
                arrive(("y", n, step, half))
                start = first_row + half * 4 * rows
                total = part_own[step, start : start + 4 * rows]
                total = (total + recv[step, half].astype(F32)).reshape(4, rows, COLS)
                for at in range(4):
                    out[2 * at + sides[half], :, columns] = total[at].astype(BF16)
    for wait in departures:
        wait()


def body(iq, ik, iv, tq, tk, tv, weight, counts, lengths):
    width = weight.shape[1]
    steps = width // COLS

    def planes(tensor):
        tensor = tensor.reshape(PLANES, SLOTS, tensor.shape[2], HD)
        return pltpu.with_memory_space_constraint(tensor, pltpu.HBM)

    img = pltpu.VMEM((PLANES, SLOTS, IT, HD), BF16)
    txt = pltpu.VMEM((PLANES, SLOTS, TT, HD), BF16)
    way_img = pltpu.VMEM((PLANES, 2, 8, IT, HD), BF16)
    way_txt = pltpu.VMEM((PLANES, 2, 8, TT, HD), BF16)
    dma = pltpu.SemaphoreType.DMA
    hbm = pl.BlockSpec(memory_space=pltpu.HBM)
    vmem = pl.BlockSpec(memory_space=pltpu.VMEM)
    return pl.pallas_call(
        kernel,
        out_shape=(
            jax.ShapeDtypeStruct((8, IT, width), BF16),
            jax.ShapeDtypeStruct((8, TT, width), BF16),
        ),
        in_specs=[hbm] * 9,
        out_specs=(vmem, vmem),
        scratch_shapes=[
            *([img, txt] * 3),
            *([img, txt] * 3),
            pltpu.VMEM((KEYS, HD), BF16),
            pltpu.VMEM((KEYS, HD), BF16),
            *([way_img, way_txt] * 2),
            pltpu.VMEM((8, 4, 2, IT, HD), BF16), pltpu.VMEM((8, 4, 2, TT, HD), BF16),
            pltpu.VMEM((SLOTS, 4, IT, HD), BF16), pltpu.VMEM((SLOTS, 4, TT, HD), BF16),
            pltpu.VMEM(weight.shape, BF16),
            pltpu.VMEM((8 * IT, 8 * HD), BF16),
            pltpu.VMEM((8 * TT, 8 * HD), BF16),
            pltpu.VMEM((8 * IT + 8 * TT, 8 * HD), BF16),
            *(
                [
                    pltpu.VMEM((steps, 2, 4 * IT, COLS), BF16),
                    pltpu.VMEM((steps, 2, 4 * TT, COLS), BF16),
                ]
                * 2
            ),
            pltpu.VMEM((steps, 8 * IT + 8 * TT, COLS), F32),
            pltpu.SMEM((16,), jnp.int32), pltpu.SMEM((16,), jnp.int32),
            *([img, txt] * 3), dma((6,)),
            dma((6,)), dma((6,)), dma((6,)), dma((6,)),
            dma((2,)), dma((2,)), dma((4,)), dma((4,)),
            dma((2, steps, 2)), dma((2, steps, 2)), dma, dma((18,)),
        ],
        compiler_params=pltpu.CompilerParams(
            collective_id=0, has_side_effects=True, vmem_limit_bytes=40 * 2**20
        ),
        cost_estimate=pl.CostEstimate(
            flops=2_500_000_000, bytes_accessed=10_000_000, transcendentals=2_400_000
        ),
        name="joint_attention",
    )(
        planes(iq), planes(ik), planes(iv), planes(tq), planes(tk), planes(tv),
        pltpu.with_memory_space_constraint(weight, pltpu.HBM),
        pltpu.with_memory_space_constraint(counts, pltpu.HBM),
        pltpu.with_memory_space_constraint(lengths, pltpu.HBM),
    )


def solution(mesh):
    tokens = P(None, "head", "seq", None)
    return jax.shard_map(
        body,
        mesh=mesh,
        in_specs=(tokens,) * 6 + (P("head", None), P(), P()),
        out_specs=(P("head", "seq", None), P("head", "seq", None)),
        check_vma=False,
    )
```

```python
import jax
import jax.numpy as jnp
from jax import lax
from jax.experimental import pallas as pl
from jax.experimental.pallas import tpu as pltpu
from jax.sharding import PartitionSpec as P

MESH = pl.DeviceIdType.MESH
BF16 = jnp.bfloat16
F32 = jnp.float32

PLANES = 8
SLOTS = 16
HD = 128
IT, TT = 8, 4
IMG_KEYS = PLANES * SLOTS * IT
TXT_KEYS = PLANES * SLOTS * TT
KEYS = IMG_KEYS + TXT_KEYS
COLS = 1024


def merge(block):
    wide = block.astype(F32)
    rows = 1
    for extent in block.shape[:-1]:
        rows *= extent
    return wide.reshape(rows, block.shape[-1]).astype(BF16)


def kernel(
    iq, ik, iv, tq, tk, tv, weight, counts_hbm, lengths_hbm,
    out_image, out_text,
    a_ik, a_tk, a_iv, a_tv, a_iq, a_tq,
    b_ik, b_tk, b_iv, b_tv, b_iq, b_tq,
    keys, values,
    s_img, s_txt, c_img, c_txt, other_img, other_txt, own_img, own_txt,
    w_vmem, lhs_img, lhs_txt, lhs_own,
    send_img, send_txt, recv_img, recv_txt, part_own,
    counts, lengths,
    v_ik, v_tk, v_iv, v_tv, v_iq, v_tq, load_sem,
    a_send, a_recv, b_send, b_recv, c_send, c_recv, d_send, d_recv,
    y_send, y_recv, w_sem, own_sem,
):
    seq = lax.axis_index("seq")
    eta = lax.axis_index("head")
    z = seq // SLOTS
    x, y, c = (seq // 4) % 4, (seq // 2) % 2, seq % 2
    pos = x * 2 + c
    slot = y * 8 + pos
    steps = weight.shape[1] // COLS

    def plane_peer(step):
        return (x + step // 4) % 4, (y + (step // 2) % 2) % 2, (c + step % 2) % 2

    def ring(step):
        return (z + 4 + (step // 2) * (2 * (step % 2) - 1)) % PLANES

    def device(plane, place):
        px, py, pc = place
        return (plane * SLOTS + px * 4 + py * 2 + pc, eta)

    here = (x, y, c)
    planes = [ring(step) for step in range(1, PLANES)]
    places = [plane_peer(step) for step in range(1, SLOTS)]
    row_places = [((x + step // 2) % 4, y, (c + step % 2) % 2) for step in range(1, 8)]

    def z_device(plane):
        return device(plane, here)

    def q_device(place):
        return device(z, place)

    def slot_of(place):
        px, py, pc = place
        return py * 8 + px * 2 + pc

    partners = ((seq, 1 - eta), (seq + 2 - 4 * y, 1 - eta))

    sources = ((ik, v_ik), (tk, v_tk), (iv, v_iv), (tv, v_tv), (tq, v_tq), (iq, v_iq))
    loads = [
        pltpu.make_async_copy(src, dst, load_sem.at[n])
        for n, (src, dst) in enumerate(sources)
    ]
    for copy in loads:
        copy.start()

    barrier = pltpu.get_barrier_semaphore()
    peers = [z_device(plane) for plane in planes]
    peers += [q_device(place) for place in places]
    peers += partners
    for peer in peers:
        pl.semaphore_signal(barrier, inc=1, device_id=peer, device_id_type=MESH)
    pl.semaphore_wait(barrier, len(peers))

    arrivals, departures = {}, []

    def remote(src, dst, send, recv, device):
        return pltpu.make_async_remote_copy(
            src_ref=src, dst_ref=dst, send_sem=send, recv_sem=recv,
            device_id=device, device_id_type=MESH,
        )

    def local(name, src, dst, sem):
        copy = pltpu.make_async_copy(src, dst, sem)
        copy.start()
        arrivals.setdefault(name, []).append(copy.wait)

    def expect(name, some, send, recv):
        copy = remote(some, some, send, recv, partners[0])
        arrivals.setdefault(name, []).append(copy.wait_recv)
        departures.append(copy.wait_send)

    def arrive(name):
        for wait in arrivals.pop(name):
            wait()


    first = ((v_ik, a_ik), (v_tk, a_tk), (v_iv, a_iv), (v_tv, a_tv), (v_tq, a_tq), (v_iq, a_iq))
    second = (b_ik, b_tk, b_iv, b_tv, b_tq, b_iq)

    def start_a(n):
        loads[n].wait()
        src, dst = first[n]
        for plane in planes:
            remote(
                src.at[plane], dst.at[z], a_send.at[n], a_recv.at[n], z_device(plane)
            ).start()
        expect(("a", n), dst.at[pl.ds(0, PLANES - 1)], a_send.at[n], a_recv.at[n])
        local(("a", n), src.at[z], dst.at[z], own_sem.at[n])

    def start_b(n):
        src, dst = first[n][1], second[n]
        for place in places:
            remote(
                src.at[:, slot_of(place)], dst.at[:, slot],
                b_send.at[n], b_recv.at[n], q_device(place),
            ).start()
        expect(("b", n), dst.at[:, pl.ds(0, SLOTS - 1)], b_send.at[n], b_recv.at[n])
        local(("b", n), src.at[:, slot], dst.at[:, slot], own_sem.at[6 + n])

    for n in range(2):
        start_a(n)
    local("weight", weight, w_vmem, w_sem)
    local("scalars", counts_hbm, counts, own_sem.at[16])
    local("scalars", lengths_hbm, lengths, own_sem.at[17])

    for n in range(4):
        arrive(("a", n))
        start_a(n + 2)
        start_b(n)

    arrive("scalars")
    image = 2 * z + y
    count, length = counts[image], lengths[image]

    def valid(extent, rows, limit):
        index = lax.broadcasted_iota(jnp.int32, (1, extent), 1)
        at = (index // rows) % SLOTS
        owner = index // (rows * SLOTS) * SLOTS + (at // 2) % 4 * 4 + at // 8 * 2 + at % 2
        return owner * rows + index % rows < limit

    bias = jnp.concatenate(
        [
            jnp.where(valid(IMG_KEYS, IT, count), 0.0, -1e30),
            jnp.where(valid(TXT_KEYS, TT, length), 0.0, -1e30),
        ],
        axis=1,
    ).astype(F32)

    arrive(("b", 0))
    keys[0:IMG_KEYS] = merge(b_ik[...])
    arrive(("b", 1))
    keys[IMG_KEYS:KEYS] = merge(b_tk[...])
    arrive(("b", 2))
    values[0:IMG_KEYS] = merge(b_iv[...])
    arrive(("b", 3))
    values[IMG_KEYS:KEYS] = merge(b_tv[...])

    factor = HD**-0.5 * 1.4426950408889634

    def attend(rows):
        scores = lax.dot_general(
            rows, keys[...], (((1,), (1,)), ((), ())), preferred_element_type=F32
        )
        scores = scores + bias
        highest = jnp.max(scores, axis=1, keepdims=True)
        powers = jnp.exp2((scores - highest) * factor)
        total = jnp.sum(powers, axis=1, keepdims=True)
        mixed = jnp.dot(powers.astype(BF16), values[...], preferred_element_type=F32)
        return mixed * (1.0 / total)

    arrive(("a", 4))
    start_b(4)
    arrive(("b", 4))
    arrive(("a", 5))
    start_b(5)

    def text_pair(planes):
        rows = [merge(b_tq[plane]) for plane in planes]
        return attend(jnp.concatenate(rows, axis=0)).reshape(2, 2, 8, TT, HD).astype(BF16)

    def send_text(plane, mixed):
        s_txt[plane] = mixed
        remote(
            s_txt.at[plane], c_txt.at[z], c_send.at[1], c_recv.at[1], z_device(plane)
        ).start()

    def text_chunk(step, carry):
        pair = [ring(2 * step + 1 + k) for k in range(2)]
        mixed = text_pair(pair)
        for k in range(2):
            send_text(pair[k], mixed[k])
        return carry

    lax.fori_loop(0, 3, text_chunk, 0)
    mixed = text_pair((planes[6], z))
    send_text(planes[6], mixed[0])
    c_txt[z] = mixed[1]
    expect(("c", 1), c_txt.at[pl.ds(0, PLANES - 1)], c_send.at[1], c_recv.at[1])

    arrive(("b", 5))

    def image_chunk(step, carry):
        plane = ring(step)
        mixed = attend(merge(b_iq[plane]))
        s_img[plane] = mixed.reshape(2, 8, IT, HD).astype(BF16)
        remote(
            s_img.at[plane], c_img.at[z], c_send.at[0], c_recv.at[0], z_device(plane)
        ).start()
        return carry

    lax.fori_loop(1, PLANES, image_chunk, 0)
    expect(("c", 0), c_img.at[pl.ds(0, PLANES - 1)], c_send.at[0], c_recv.at[0])
    c_img[z] = attend(merge(b_iq[z])).reshape(2, 8, IT, HD).astype(BF16)

    mine, others = pl.ds(4 * eta, 4), pl.ds(4 - 4 * eta, 4)
    spread = ((c_img, other_img, own_img), (c_txt, other_txt, own_txt))
    for n in (1, 0):
        src, other, own = spread[n]
        arrive(("c", n))
        for place in row_places:
            remote(
                src.at[others, :, place[0] * 2 + place[2]], other.at[pos],
                d_send.at[n], d_recv.at[n], q_device(place),
            ).start()
        expect(("d", n), other.at[pl.ds(0, 7)], d_send.at[n], d_recv.at[n])
        local(("d", n), src.at[others, :, pos], other.at[pos], own_sem.at[12 + n])
        for place in places:
            remote(
                src.at[mine, place[1], place[0] * 2 + place[2]], own.at[slot],
                d_send.at[2 + n], d_recv.at[2 + n], q_device(place),
            ).start()
        expect(("d", 2 + n), own.at[pl.ds(0, SLOTS - 1)], d_send.at[2 + n], d_recv.at[2 + n])
        local(("d", 2 + n), src.at[mine, y, pos], own.at[slot], own_sem.at[14 + n])

    arrive("weight")
    sides = (y, 1 - y)
    partial = (
        (other_img, lhs_img, send_img, recv_img), (other_txt, lhs_txt, send_txt, recv_txt)
    )
    for n in (1, 0):
        other, lhs, send, recv = partial[n]
        height = lhs.shape[0] // 2
        arrive(("d", n))
        for half in range(2):
            for head in range(8):
                lhs[
                    half * height : (half + 1) * height, head * HD : (head + 1) * HD
                ] = merge(other[head, :, sides[half]])
        for step in range(steps):
            columns = pl.ds(step * COLS, COLS)
            part = jnp.dot(lhs[...], w_vmem[:, columns], preferred_element_type=F32)
            send[step] = part.astype(BF16).reshape(2, height, COLS)
            for half, partner in enumerate(partners):
                copy = remote(
                    send.at[step, half], recv.at[step, half],
                    y_send.at[n, step, half], y_recv.at[n, step, half], partner,
                )
                copy.start()
                arrivals[("y", n, step, half)] = [copy.wait_recv]
                departures.append(copy.wait_send)

    for n, (own, first_row, height) in enumerate(((own_img, 0, 4 * IT), (own_txt, 8 * IT, 4 * TT))):
        arrive(("d", 2 + n))
        for half in range(2):
            start = first_row + half * height
            for head in range(8):
                lhs_own[start : start + height, head * HD : (head + 1) * HD] = merge(
                    own[sides[half] * 8 + head]
                )
    for step in range(steps):
        columns = pl.ds(step * COLS, COLS)
        part_own[step] = jnp.dot(lhs_own[...], w_vmem[:, columns], preferred_element_type=F32)

    last = ((recv_img, out_image, 0, IT), (recv_txt, out_text, 8 * IT, TT))
    for n in (1, 0):
        recv, out, first_row, rows = last[n]
        for step in range(steps):
            columns = pl.ds(step * COLS, COLS)
            for half in range(2):
                arrive(("y", n, step, half))
                start = first_row + half * 4 * rows
                total = part_own[step, start : start + 4 * rows]
                total = (total + recv[step, half].astype(F32)).reshape(4, rows, COLS)
                for at in range(4):
                    out[2 * at + sides[half], :, columns] = total[at].astype(BF16)
    for wait in departures:
        wait()


def body(iq, ik, iv, tq, tk, tv, weight, counts, lengths):
    width = weight.shape[1]
    steps = width // COLS

    def planes(tensor):
        tensor = tensor.reshape(PLANES, SLOTS, tensor.shape[2], HD)
        return pltpu.with_memory_space_constraint(tensor, pltpu.HBM)

    img = pltpu.VMEM((PLANES, SLOTS, IT, HD), BF16)
    txt = pltpu.VMEM((PLANES, SLOTS, TT, HD), BF16)
    way_img = pltpu.VMEM((PLANES, 2, 8, IT, HD), BF16)
    way_txt = pltpu.VMEM((PLANES, 2, 8, TT, HD), BF16)
    dma = pltpu.SemaphoreType.DMA
    hbm = pl.BlockSpec(memory_space=pltpu.HBM)
    vmem = pl.BlockSpec(memory_space=pltpu.VMEM)
    return pl.pallas_call(
        kernel,
        out_shape=(
            jax.ShapeDtypeStruct((8, IT, width), BF16),
            jax.ShapeDtypeStruct((8, TT, width), BF16),
        ),
        in_specs=[hbm] * 9,
        out_specs=(vmem, vmem),
        scratch_shapes=[
            *([img, txt] * 3),
            *([img, txt] * 3),
            pltpu.VMEM((KEYS, HD), BF16),
            pltpu.VMEM((KEYS, HD), BF16),
            *([way_img, way_txt] * 2),
            pltpu.VMEM((8, 4, 2, IT, HD), BF16), pltpu.VMEM((8, 4, 2, TT, HD), BF16),
            pltpu.VMEM((SLOTS, 4, IT, HD), BF16), pltpu.VMEM((SLOTS, 4, TT, HD), BF16),
            pltpu.VMEM(weight.shape, BF16),
            pltpu.VMEM((8 * IT, 8 * HD), BF16),
            pltpu.VMEM((8 * TT, 8 * HD), BF16),
            pltpu.VMEM((8 * IT + 8 * TT, 8 * HD), BF16),
            *(
                [
                    pltpu.VMEM((steps, 2, 4 * IT, COLS), BF16),
                    pltpu.VMEM((steps, 2, 4 * TT, COLS), BF16),
                ]
                * 2
            ),
            pltpu.VMEM((steps, 8 * IT + 8 * TT, COLS), F32),
            pltpu.SMEM((16,), jnp.int32), pltpu.SMEM((16,), jnp.int32),
            *([img, txt] * 3), dma((6,)),
            dma((6,)), dma((6,)), dma((6,)), dma((6,)),
            dma((2,)), dma((2,)), dma((4,)), dma((4,)),
            dma((2, steps, 2)), dma((2, steps, 2)), dma, dma((18,)),
        ],
        compiler_params=pltpu.CompilerParams(
            collective_id=0, has_side_effects=True, vmem_limit_bytes=40 * 2**20
        ),
        cost_estimate=pl.CostEstimate(
            flops=2_500_000_000, bytes_accessed=10_000_000, transcendentals=2_400_000
        ),
        name="joint_attention",
    )(
        planes(iq), planes(ik), planes(iv), planes(tq), planes(tk), planes(tv),
        pltpu.with_memory_space_constraint(weight, pltpu.HBM),
        pltpu.with_memory_space_constraint(counts, pltpu.HBM),
        pltpu.with_memory_space_constraint(lengths, pltpu.HBM),
    )


def solution(mesh):
    tokens = P(None, "head", "seq", None)
    return jax.shard_map(
        body,
        mesh=mesh,
        in_specs=(tokens,) * 6 + (P("head", None), P(), P()),
        out_specs=(P("head", "seq", None), P("head", "seq", None)),
        check_vma=False,
    )
```

```python
import jax
import jax.numpy as jnp
from jax import lax
from jax.experimental import pallas as pl
from jax.experimental.pallas import tpu as pltpu
from jax.sharding import PartitionSpec as P

MESH = pl.DeviceIdType.MESH
BF16 = jnp.bfloat16
F32 = jnp.float32

PLANES = 8
SLOTS = 16
HD = 128
IT, TT = 8, 4
IMG_KEYS = PLANES * SLOTS * IT
TXT_KEYS = PLANES * SLOTS * TT
KEYS = IMG_KEYS + TXT_KEYS
COLS = 1024


def merge(block):
    wide = block.astype(F32)
    rows = 1
    for extent in block.shape[:-1]:
        rows *= extent
    return wide.reshape(rows, block.shape[-1]).astype(BF16)


def kernel(
    iq, ik, iv, tq, tk, tv, weight, counts_hbm, lengths_hbm,
    out_image, out_text,
    a_ik, a_tk, a_iv, a_tv, a_iq, a_tq,
    b_ik, b_tk, b_iv, b_tv, b_iq, b_tq,
    keys, values,
    s_img, s_txt, c_img, c_txt, other_img, other_txt, own_img, own_txt,
    w_vmem, lhs_img, lhs_txt, lhs_own,
    send_img, send_txt, recv_img, recv_txt, part_own,
    counts, lengths,
    v_ik, v_tk, v_iv, v_tv, v_iq, v_tq, load_sem,
    a_send, a_recv, b_send, b_recv, c_send, c_recv, d_send, d_recv,
    y_send, y_recv, w_sem, own_sem,
):
    seq = lax.axis_index("seq")
    eta = lax.axis_index("head")
    z = seq // SLOTS
    x, y, c = (seq // 4) % 4, (seq // 2) % 2, seq % 2
    pos = x * 2 + c
    slot = y * 8 + pos
    steps = weight.shape[1] // COLS

    def plane_peer(step):
        return (x + step // 4) % 4, (y + (step // 2) % 2) % 2, (c + step % 2) % 2

    def ring(step):
        return (z + 4 + (step // 2) * (2 * (step % 2) - 1)) % PLANES

    def device(plane, place):
        px, py, pc = place
        return (plane * SLOTS + px * 4 + py * 2 + pc, eta)

    here = (x, y, c)
    planes = [ring(step) for step in range(1, PLANES)]
    places = [plane_peer(step) for step in range(1, SLOTS)]
    row_places = [((x + step // 2) % 4, y, (c + step % 2) % 2) for step in range(1, 8)]

    def z_device(plane):
        return device(plane, here)

    def q_device(place):
        return device(z, place)

    def slot_of(place):
        px, py, pc = place
        return py * 8 + px * 2 + pc

    partners = ((seq, 1 - eta), (seq + 2 - 4 * y, 1 - eta))

    sources = ((ik, v_ik), (tk, v_tk), (iv, v_iv), (tv, v_tv), (tq, v_tq), (iq, v_iq))
    loads = [
        pltpu.make_async_copy(src, dst, load_sem.at[n])
        for n, (src, dst) in enumerate(sources)
    ]
    for copy in loads:
        copy.start()

    barrier = pltpu.get_barrier_semaphore()
    peers = [z_device(plane) for plane in planes]
    peers += [q_device(place) for place in places]
    peers += partners
    for peer in peers:
        pl.semaphore_signal(barrier, inc=1, device_id=peer, device_id_type=MESH)
    pl.semaphore_wait(barrier, len(peers))

    arrivals, departures = {}, []

    def remote(src, dst, send, recv, device):
        return pltpu.make_async_remote_copy(
            src_ref=src, dst_ref=dst, send_sem=send, recv_sem=recv,
            device_id=device, device_id_type=MESH,
        )

    def local(name, src, dst, sem):
        copy = pltpu.make_async_copy(src, dst, sem)
        copy.start()
        arrivals.setdefault(name, []).append(copy.wait)

    def expect(name, some, send, recv):
        copy = remote(some, some, send, recv, partners[0])
        arrivals.setdefault(name, []).append(copy.wait_recv)
        departures.append(copy.wait_send)

    def arrive(name):
        for wait in arrivals.pop(name):
            wait()


    first = ((v_ik, a_ik), (v_tk, a_tk), (v_iv, a_iv), (v_tv, a_tv), (v_tq, a_tq), (v_iq, a_iq))
    second = (b_ik, b_tk, b_iv, b_tv, b_tq, b_iq)

    def start_a(n):
        loads[n].wait()
        src, dst = first[n]
        for plane in planes:
            remote(
                src.at[plane], dst.at[z], a_send.at[n], a_recv.at[n], z_device(plane)
            ).start()
        expect(("a", n), dst.at[pl.ds(0, PLANES - 1)], a_send.at[n], a_recv.at[n])
        local(("a", n), src.at[z], dst.at[z], own_sem.at[n])

    def start_b(n):
        src, dst = first[n][1], second[n]
        for place in places:
            remote(
                src.at[:, slot_of(place)], dst.at[:, slot],
                b_send.at[n], b_recv.at[n], q_device(place),
            ).start()
        expect(("b", n), dst.at[:, pl.ds(0, SLOTS - 1)], b_send.at[n], b_recv.at[n])
        local(("b", n), src.at[:, slot], dst.at[:, slot], own_sem.at[6 + n])

    for n in range(2):
        start_a(n)
    local("weight", weight, w_vmem, w_sem)
    local("scalars", counts_hbm, counts, own_sem.at[16])
    local("scalars", lengths_hbm, lengths, own_sem.at[17])

    for n in range(4):
        arrive(("a", n))
        start_a(n + 2)
        start_b(n)

    arrive("scalars")
    image = 2 * z + y
    count, length = counts[image], lengths[image]

    def valid(extent, rows, limit):
        index = lax.broadcasted_iota(jnp.int32, (1, extent), 1)
        at = (index // rows) % SLOTS
        owner = index // (rows * SLOTS) * SLOTS + (at // 2) % 4 * 4 + at // 8 * 2 + at % 2
        return owner * rows + index % rows < limit

    bias = jnp.concatenate(
        [
            jnp.where(valid(IMG_KEYS, IT, count), 0.0, -1e30),
            jnp.where(valid(TXT_KEYS, TT, length), 0.0, -1e30),
        ],
        axis=1,
    ).astype(F32)

    arrive(("b", 0))
    keys[0:IMG_KEYS] = merge(b_ik[...])
    arrive(("b", 1))
    keys[IMG_KEYS:KEYS] = merge(b_tk[...])
    arrive(("b", 2))
    values[0:IMG_KEYS] = merge(b_iv[...])
    arrive(("b", 3))
    values[IMG_KEYS:KEYS] = merge(b_tv[...])

    factor = HD**-0.5 * 1.4426950408889634

    def attend(rows):
        scores = lax.dot_general(
            rows, keys[...], (((1,), (1,)), ((), ())), preferred_element_type=F32
        )
        scores = scores + bias
        highest = jnp.max(scores, axis=1, keepdims=True)
        powers = jnp.exp2((scores - highest) * factor)
        total = jnp.sum(powers, axis=1, keepdims=True)
        mixed = jnp.dot(powers.astype(BF16), values[...], preferred_element_type=F32)
        return mixed * (1.0 / total)

    arrive(("a", 4))
    start_b(4)
    arrive(("a", 5))
    start_b(5)
    arrive(("b", 4))

    def text_pair(planes):
        rows = [merge(b_tq[plane]) for plane in planes]
        return attend(jnp.concatenate(rows, axis=0)).reshape(2, 2, 8, TT, HD).astype(BF16)

    def send_text(plane, mixed):
        s_txt[plane] = mixed
        remote(
            s_txt.at[plane], c_txt.at[z], c_send.at[1], c_recv.at[1], z_device(plane)
        ).start()

    def text_chunk(step, carry):
        pair = [ring(2 * step + 1 + k) for k in range(2)]
        mixed = text_pair(pair)
        for k in range(2):
            send_text(pair[k], mixed[k])
        return carry

    lax.fori_loop(0, 3, text_chunk, 0)
    mixed = text_pair((planes[6], z))
    send_text(planes[6], mixed[0])
    c_txt[z] = mixed[1]
    expect(("c", 1), c_txt.at[pl.ds(0, PLANES - 1)], c_send.at[1], c_recv.at[1])

    arrive(("b", 5))

    def image_chunk(step, carry):
        plane = ring(step)
        mixed = attend(merge(b_iq[plane]))
        s_img[plane] = mixed.reshape(2, 8, IT, HD).astype(BF16)
        remote(
            s_img.at[plane], c_img.at[z], c_send.at[0], c_recv.at[0], z_device(plane)
        ).start()
        return carry

    lax.fori_loop(1, PLANES, image_chunk, 0)
    expect(("c", 0), c_img.at[pl.ds(0, PLANES - 1)], c_send.at[0], c_recv.at[0])
    c_img[z] = attend(merge(b_iq[z])).reshape(2, 8, IT, HD).astype(BF16)

    mine, others = pl.ds(4 * eta, 4), pl.ds(4 - 4 * eta, 4)
    spread = ((c_img, other_img, own_img), (c_txt, other_txt, own_txt))
    for n in (1, 0):
        src, other, own = spread[n]
        arrive(("c", n))
        for place in row_places:
            remote(
                src.at[others, :, place[0] * 2 + place[2]], other.at[pos],
                d_send.at[n], d_recv.at[n], q_device(place),
            ).start()
        expect(("d", n), other.at[pl.ds(0, 7)], d_send.at[n], d_recv.at[n])
        local(("d", n), src.at[others, :, pos], other.at[pos], own_sem.at[12 + n])
        for place in places:
            remote(
                src.at[mine, place[1], place[0] * 2 + place[2]], own.at[slot],
                d_send.at[2 + n], d_recv.at[2 + n], q_device(place),
            ).start()
        expect(("d", 2 + n), own.at[pl.ds(0, SLOTS - 1)], d_send.at[2 + n], d_recv.at[2 + n])
        local(("d", 2 + n), src.at[mine, y, pos], own.at[slot], own_sem.at[14 + n])

    arrive("weight")
    sides = (y, 1 - y)
    partial = (
        (other_img, lhs_img, send_img, recv_img), (other_txt, lhs_txt, send_txt, recv_txt)
    )
    for n in (1, 0):
        other, lhs, send, recv = partial[n]
        height = lhs.shape[0] // 2
        arrive(("d", n))
        for half in range(2):
            for head in range(8):
                lhs[
                    half * height : (half + 1) * height, head * HD : (head + 1) * HD
                ] = merge(other[head, :, sides[half]])
        for step in range(steps):
            columns = pl.ds(step * COLS, COLS)
            part = jnp.dot(lhs[...], w_vmem[:, columns], preferred_element_type=F32)
            send[step] = part.astype(BF16).reshape(2, height, COLS)
            for half, partner in enumerate(partners):
                copy = remote(
                    send.at[step, half], recv.at[step, half],
                    y_send.at[n, step, half], y_recv.at[n, step, half], partner,
                )
                copy.start()
                arrivals[("y", n, step, half)] = [copy.wait_recv]
                departures.append(copy.wait_send)

    for n, (own, first_row, height) in enumerate(((own_img, 0, 4 * IT), (own_txt, 8 * IT, 4 * TT))):
        arrive(("d", 2 + n))
        for half in range(2):
            start = first_row + half * height
            for head in range(8):
                lhs_own[start : start + height, head * HD : (head + 1) * HD] = merge(
                    own[sides[half] * 8 + head]
                )
    for step in range(steps):
        columns = pl.ds(step * COLS, COLS)
        part_own[step] = jnp.dot(lhs_own[...], w_vmem[:, columns], preferred_element_type=F32)

    last = ((recv_img, out_image, 0, IT), (recv_txt, out_text, 8 * IT, TT))
    for n in (1, 0):
        recv, out, first_row, rows = last[n]
        for step in range(steps):
            columns = pl.ds(step * COLS, COLS)
            for half in range(2):
                arrive(("y", n, step, half))
                start = first_row + half * 4 * rows
                total = part_own[step, start : start + 4 * rows]
                total = (total + recv[step, half].astype(F32)).reshape(4, rows, COLS)
                for at in range(4):
                    out[2 * at + sides[half], :, columns] = total[at].astype(BF16)
    for wait in departures:
        wait()


def body(iq, ik, iv, tq, tk, tv, weight, counts, lengths):
    width = weight.shape[1]
    steps = width // COLS

    def planes(tensor):
        tensor = tensor.reshape(PLANES, SLOTS, tensor.shape[2], HD)
        return pltpu.with_memory_space_constraint(tensor, pltpu.HBM)

    img = pltpu.VMEM((PLANES, SLOTS, IT, HD), BF16)
    txt = pltpu.VMEM((PLANES, SLOTS, TT, HD), BF16)
    way_img = pltpu.VMEM((PLANES, 2, 8, IT, HD), BF16)
    way_txt = pltpu.VMEM((PLANES, 2, 8, TT, HD), BF16)
    dma = pltpu.SemaphoreType.DMA
    hbm = pl.BlockSpec(memory_space=pltpu.HBM)
    vmem = pl.BlockSpec(memory_space=pltpu.VMEM)
    return pl.pallas_call(
        kernel,
        out_shape=(
            jax.ShapeDtypeStruct((8, IT, width), BF16),
            jax.ShapeDtypeStruct((8, TT, width), BF16),
        ),
        in_specs=[hbm] * 9,
        out_specs=(vmem, vmem),
        scratch_shapes=[
            *([img, txt] * 3),
            *([img, txt] * 3),
            pltpu.VMEM((KEYS, HD), BF16),
            pltpu.VMEM((KEYS, HD), BF16),
            *([way_img, way_txt] * 2),
            pltpu.VMEM((8, 4, 2, IT, HD), BF16), pltpu.VMEM((8, 4, 2, TT, HD), BF16),
            pltpu.VMEM((SLOTS, 4, IT, HD), BF16), pltpu.VMEM((SLOTS, 4, TT, HD), BF16),
            pltpu.VMEM(weight.shape, BF16),
            pltpu.VMEM((8 * IT, 8 * HD), BF16),
            pltpu.VMEM((8 * TT, 8 * HD), BF16),
            pltpu.VMEM((8 * IT + 8 * TT, 8 * HD), BF16),
            *(
                [
                    pltpu.VMEM((steps, 2, 4 * IT, COLS), BF16),
                    pltpu.VMEM((steps, 2, 4 * TT, COLS), BF16),
                ]
                * 2
            ),
            pltpu.VMEM((steps, 8 * IT + 8 * TT, COLS), F32),
            pltpu.SMEM((16,), jnp.int32), pltpu.SMEM((16,), jnp.int32),
            *([img, txt] * 3), dma((6,)),
            dma((6,)), dma((6,)), dma((6,)), dma((6,)),
            dma((2,)), dma((2,)), dma((4,)), dma((4,)),
            dma((2, steps, 2)), dma((2, steps, 2)), dma, dma((18,)),
        ],
        compiler_params=pltpu.CompilerParams(
            collective_id=0, has_side_effects=True, vmem_limit_bytes=40 * 2**20
        ),
        cost_estimate=pl.CostEstimate(
            flops=2_500_000_000, bytes_accessed=10_000_000, transcendentals=2_400_000
        ),
        name="joint_attention",
    )(
        planes(iq), planes(ik), planes(iv), planes(tq), planes(tk), planes(tv),
        pltpu.with_memory_space_constraint(weight, pltpu.HBM),
        pltpu.with_memory_space_constraint(counts, pltpu.HBM),
        pltpu.with_memory_space_constraint(lengths, pltpu.HBM),
    )


def solution(mesh):
    tokens = P(None, "head", "seq", None)
    return jax.shard_map(
        body,
        mesh=mesh,
        in_specs=(tokens,) * 6 + (P("head", None), P(), P()),
        out_specs=(P("head", "seq", None), P("head", "seq", None)),
        check_vma=False,
    )
```
